32 devices in a mesh: dp: 4 (over y, core), expert: 8 (over z, x).
Axes of the slice: x: 2, y: 2, z: 4, core: 2. Of those that a mesh axis runs over, the one named last changes fastest.
Arguments:
- tokens: bfloat16 [4096, 2048], P(('dp', 'expert')), may hold values from -9 to 9
- out_grad: bfloat16 [4096, 2048], P(('dp', 'expert')), may hold values from -1.8 to 1.8
- probs: bfloat16 [4096, 8], P(('dp', 'expert')), may hold values from 0.019897461 to 0.5
- expert_ids: int32 [4096, 8], P(('dp', 'expert')), may hold values from 0 to 31, all different within a row; in each aligned block of 128 rows (0 to 127, 128 to 255, ...) at most 40 rows name the same one
- dropped: int32 [4096, 8], P(('dp', 'expert')), may hold values 0 or 1
- preacts: bfloat16 [4, 32, 320, 768], P('dp', 'expert'), may hold values from -6 to 6
- w_gu: bfloat16 [32, 2048, 768], P('expert', 'dp'), may hold values from -0.125 to 0.125
- w_down: bfloat16 [32, 384, 2048], P('expert', None, 'dp'), may hold values from -0.3125 to 0.3125
Outputs:
- tok_grad: bfloat16 [4096, 2048], P(('dp', 'expert'))
- prob_grad: bfloat16 [4096, 8], P(('dp', 'expert'))
- grad_gu: float32 [32, 2048, 768], P('expert', 'dp')
- grad_down: float32 [32, 384, 2048], P('expert', None, 'dp')
- mean_square: float32 [], replicated
The draws below stay inside these ranges and needn't reach their ends.
Inputs may be any that keep to these rules, and one draw needn't show every extreme that they name: `expert_ids`: each row names 8 different experts. Within the rows of one device no expert is named more than 40 times, a bound that some block reaches in every draw.
All inputs are finite; a program needn't handle non-finite values. No bound on the sum of `dropped` on one device may be relied on, other than what follows from the above.
Results may differ from the reference program's by a relative error of at most 0.017.
Values may be sent and summed in bfloat16 or wider, within the bound.
A program may use at most 128 MiB of HBM per device.

```python
import math
import jax
import jax.numpy as jnp
import numpy as np
from jax import lax

D = 2048
TOP = 8
FW = 384
EXPERTS = 32
TOK_DEV = 128
CAP = 40
SLOTS = 320
TOKENS = 4096
N_DP = 4
N_EXPERT = 8


def column_scale(low):
    return low + jnp.arange(D, dtype=jnp.float32) / (D - 1)


def draw_tokens(key, part):
    key = jax.random.fold_in(key, 11)
    values = jnp.clip(jax.random.normal(key, (TOKENS, D), jnp.float32), -6.0, 6.0) * column_scale(0.5)[None, :]
    return values.astype(jnp.bfloat16)


def draw_out_grad(key, part):
    key = jax.random.fold_in(key, 23)
    values = 0.3 * jnp.clip(jax.random.normal(key, (TOKENS, D), jnp.float32), -4.0, 4.0) * column_scale(0.5)[None, :]
    return values.astype(jnp.bfloat16)


def touch_ends(values, key, smallest, top_value):
    dims = values.shape
    place = [jax.random.randint(jax.random.fold_in(key, axis), (), 0, dims[axis]) for axis in range(len(dims))]
    values = values.at[tuple(place)].set(smallest)
    longest = dims.index(max(dims))
    place[longest] = (place[longest] + 1) % dims[longest]
    return values.at[tuple(place)].set(top_value)


def shard_levels(own_key, shape, pieces, smallest, largest):
    gain = 1.0
    for dim, shards_of in pieces:
        draws = jax.random.uniform(jax.random.fold_in(jax.random.fold_in(own_key, 6), dim), (shards_of,), jnp.float32, smallest / len(pieces), largest / len(pieces))
        gain = gain * jnp.repeat(jnp.exp(draws), shape[dim] // shards_of).reshape((-1,) + (1,) * (len(shape) - 1 - dim))
    return gain


def deal_out(own_key, own, number, rows, count, top, bound, slope):
    sequence = jax.random.permutation(own_key, count)
    crowded, usual = shares(count, rows * top, bound, slope, True), shares(count, rows * top, bound, slope, False)
    places = jnp.arange(count)

    def named(sizes, turn):
        used = int((sizes > 0).sum())
        fixed = max(1, used // 4)
        moved = fixed + (places - fixed + turn * (used - fixed)) % max(1, count - fixed)
        return jnp.zeros((count,), jnp.int32).at[sequence[jnp.where(places < fixed, places, moved)]].set(jnp.asarray(sizes, jnp.int32))

    sizes = jnp.where(number % 4 == 0, named(crowded, number // 4), named(usual, number - number // 4 - 1))
    mixed = jax.random.permutation(jax.random.fold_in(own, 3), count)
    giver, receiver = mixed[0:count // 2 * 2:2], mixed[1:count // 2 * 2:2]
    room = jnp.minimum(sizes[giver] - 1, bound - sizes[receiver]) // 2
    room = jnp.where((giver == sequence[0]) | (receiver == sequence[0]) | (sizes[receiver] == 0), 0, jnp.maximum(room, 0))
    moved = jax.random.randint(jax.random.fold_in(own, 4), (count // 2,), 0, 1 << 20) % (room + 1)
    sizes = sizes.at[giver].add(-moved).at[receiver].add(moved)
    items = jnp.searchsorted(jnp.cumsum(sizes), jnp.arange(rows * top), side="right").astype(jnp.int32)
    grid = items.reshape(top, rows).T
    grid = grid[jax.random.permutation(jax.random.fold_in(own, 1), rows)]
    turn = jax.random.randint(jax.random.fold_in(own, 2), (rows, 1), 0, top)
    return jnp.take_along_axis(grid, (jnp.arange(top)[None, :] + turn) % top, axis=1)


def shares(count, total, reach, lean, full):
    loads = [(1 << 20) // math.isqrt(rank ** lean) + 1 for rank in range(1, count + 1)]
    largest = reach if full else min(reach, max(-(-total // count), total * loads[0] // sum(loads)))
    least = 1 if total - largest >= count - 1 else 0
    holding, spare = [largest] + [least] * (count - 1), total - largest - least * (count - 1)
    while spare > 0:
        free = [i for i in range(1, count) if holding[i] < largest] or [i for i in range(1, count) if holding[i] < reach]
        mass, budget = sum([loads[i] for i in free]), spare
        for i in free:
            addition = min(reach - holding[i], max(1, budget * loads[i] // mass), spare)
            holding[i] = holding[i] + addition
            spare = spare - addition
    return np.array(holding)


def centred(key, shape, scale, limit, shards=(), kind=jnp.bfloat16):
    values = scale * jax.random.normal(key, shape, jnp.float32)
    if shards:
        values = values * shard_levels(key, shape, shards, -0.22, 0.18)
    return jnp.clip(values, -limit, limit).astype(kind)


def setup_inputs(seed: int = 0) -> dict:
    splits = jax.random.split(jax.random.key(seed), 9)
    tokens = draw_tokens(jax.random.fold_in(splits[8], 71), 0)
    out_grad = draw_out_grad(jax.random.fold_in(splits[8], 71), 0)
    probs = jnp.clip(jnp.exp(math.log(0.5) - 3.224016 * jax.random.uniform(splits[2], (TOKENS, TOP), jnp.float32) ** shard_levels(splits[2], (TOKENS, TOP), ((0, 32),), -0.2, 0.2)), 0.019897461, 0.5).astype(jnp.bfloat16)
    expert_ids_keys = jax.random.split(jax.random.fold_in(splits[3], 1), TOKENS // TOK_DEV)
    expert_ids_turns = jax.random.permutation(jax.random.fold_in(splits[3], 3), TOKENS // TOK_DEV)
    expert_ids = jax.vmap(lambda own, number: deal_out(jax.random.fold_in(splits[3], 2), own, number, TOK_DEV, EXPERTS, TOP, CAP, 2))(expert_ids_keys, expert_ids_turns).reshape((TOKENS, TOP))
    dropped = touch_ends((jax.random.randint(splits[4], (TOKENS, TOP), 0, 8) < 1).astype(jnp.int32), jax.random.fold_in(splits[4], 1), 0, 1)
    preacts = centred(splits[5], (N_DP, EXPERTS, SLOTS, 2 * FW), 1.0, 6.0, ((0, 4), (1, 8)))
    w_gu = centred(splits[6], (EXPERTS, D, 2 * FW), D ** -0.5, 0.125, ((0, 8), (1, 4)))
    w_down = centred(splits[7], (EXPERTS, FW, D), FW ** -0.5, 0.3125, ((0, 8), (2, 4)))
    return dict(tokens=tokens, out_grad=out_grad, probs=probs, expert_ids=expert_ids, dropped=dropped, preacts=preacts, w_gu=w_gu, w_down=w_down)


def slot_match(expert_ids, dropped, experts, capacity):
    tok_rows, top_k = expert_ids.shape
    flat_ids = expert_ids.reshape(-1)
    onehot = (flat_ids[:, None] == jnp.arange(experts, dtype=jnp.int32)[None, :]).astype(jnp.int32)
    before = jnp.cumsum(onehot, axis=0) - onehot
    position = jnp.sum(before * onehot, axis=1).astype(jnp.int32)
    slot_ids = flat_ids * capacity + position
    slot_ids = jnp.where(dropped.reshape(-1) == 0, slot_ids, -1).reshape(tok_rows, top_k)
    every_slot = jnp.arange(experts * capacity, dtype=jnp.int32)
    return (every_slot[:, None, None] == slot_ids[None, :, :]).astype(jnp.float32)


def reference(tokens, out_grad, probs, expert_ids, dropped, preacts, w_gu, w_down):
    w_gu_f = w_gu.astype(jnp.float32)
    w_down_f = w_down.astype(jnp.float32)

    def row_pass(carry, row_data):
        tokens_row, grad_row, probs_row, ids_row, drop_row, pre_row = row_data
        matches = jax.vmap(slot_match, in_axes=(0, 0, None, None))(ids_row, drop_row, EXPERTS, CAP)
        counts = jnp.sum(matches, axis=3)
        x_in = jnp.einsum('jqt,jtd->jqd', counts, tokens_row.astype(jnp.float32)).astype(jnp.bfloat16)
        grad_in = jnp.einsum('jqt,jtd->jqd', counts, grad_row.astype(jnp.float32)).astype(jnp.bfloat16)
        x_in = x_in.reshape(N_EXPERT, EXPERTS, CAP, D)
        grad_in = grad_in.reshape(N_EXPERT, EXPERTS, CAP, D)
        prob_in = jnp.einsum('jqtk,jtk->jq', matches, probs_row.astype(jnp.float32)).astype(jnp.bfloat16)
        prob_in = prob_in.reshape(N_EXPERT, EXPERTS, CAP)
        pre_acts = pre_row.reshape(EXPERTS, N_EXPERT, CAP, 2 * FW).astype(jnp.float32)
        proj = jnp.einsum('jecd,efd->ejcf', grad_in.astype(jnp.float32), w_down_f)
        gate_pre = pre_acts[..., :FW]
        up_pre = pre_acts[..., FW:]
        sigmoid_a = jax.nn.sigmoid(gate_pre)
        silu_a = gate_pre * sigmoid_a
        hidden = silu_a * up_pre
        slot_prob = jnp.sum(hidden * proj, axis=-1).astype(jnp.bfloat16)
        weight_p = jnp.transpose(prob_in, (1, 0, 2)).astype(jnp.float32)[..., None]
        scaled = weight_p * proj
        dgu = jnp.concatenate([scaled * up_pre * sigmoid_a * (1.0 + gate_pre * (1.0 - sigmoid_a)), scaled * silu_a], axis=-1).astype(jnp.bfloat16)
        slot_grad = jnp.einsum('ejcf,edf->jecd', dgu.astype(jnp.float32), w_gu_f).astype(jnp.bfloat16)
        hidden_p = (weight_p * hidden).astype(jnp.bfloat16)
        grad_gu_row = jnp.einsum('jecd,ejcf->edf', x_in.astype(jnp.float32), dgu.astype(jnp.float32))
        grad_down_row = jnp.einsum('ejcf,jecd->efd', hidden_p.astype(jnp.float32), grad_in.astype(jnp.float32))
        slot_flat = slot_grad.reshape(N_EXPERT, EXPERTS * CAP, D).astype(jnp.float32)
        tok_grad_row = jnp.einsum('jqt,jqd->jtd', counts, slot_flat).astype(jnp.bfloat16)
        prob_slot = jnp.transpose(slot_prob, (1, 0, 2)).reshape(N_EXPERT, EXPERTS * CAP).astype(jnp.float32)
        prob_grad_row = jnp.einsum('jqtk,jq->jtk', matches, prob_slot).astype(jnp.bfloat16)
        return (carry[0] + grad_gu_row, carry[1] + grad_down_row), (tok_grad_row, prob_grad_row)

    start = (jnp.zeros((EXPERTS, D, 2 * FW), jnp.float32), jnp.zeros((EXPERTS, FW, D), jnp.float32))
    row_inputs = (tokens.reshape(N_DP, N_EXPERT, TOK_DEV, D), out_grad.reshape(N_DP, N_EXPERT, TOK_DEV, D),
                  probs.reshape(N_DP, N_EXPERT, TOK_DEV, TOP), expert_ids.reshape(N_DP, N_EXPERT, TOK_DEV, TOP),
                  dropped.reshape(N_DP, N_EXPERT, TOK_DEV, TOP), preacts)
    (grad_gu, grad_down), (tok_grad, prob_grad) = lax.scan(row_pass, start, row_inputs)
    total = jnp.sum(grad_gu * grad_gu) + jnp.sum(grad_down * grad_down)
    mean_square = total / (EXPERTS * 3 * D * FW)
    return (tok_grad.reshape(TOKENS, D), prob_grad.reshape(TOKENS, TOP), grad_gu, grad_down, mean_square)
```

```python
import jax
import jax.numpy as jnp
from jax import lax
from jax.sharding import PartitionSpec as P

EXPERTS = 32
CAP = 40
BF = jnp.bfloat16
F32 = jnp.float32


def xor_permute(x, axis, bit):
    n = lax.axis_size(axis)
    return lax.ppermute(x, axis, [(a, a ^ bit) for a in range(n)])


def gather_rel(x, axis):
    n = lax.axis_size(axis)
    buf = x[None]
    bit = n // 2
    while bit:
        other = xor_permute(buf, axis, bit)
        buf = jnp.stack([buf, other], axis=1).reshape((-1,) + x.shape)
        bit //= 2
    return buf


def scatter_rel(x, axis, wire):
    n = lax.axis_size(axis)
    bit = 1
    while bit < n:
        got = xor_permute(x[1::2].astype(wire), axis, bit)
        x = x[0::2].astype(F32) + got.astype(F32)
        bit *= 2
    return x[0]


def swap_rel(pieces, axis):
    return [pieces[0]] + [xor_permute(pieces[r], axis, r) for r in range(1, len(pieces))]


def body(tokens, out_grad, probs, expert_ids, dropped, preacts, w_gu, w_down):
    n_dp, n_ex = lax.axis_size("dp"), lax.axis_size("expert")
    local = EXPERTS // n_ex
    rows, width = tokens.shape
    top = probs.shape[1]
    part = width // n_dp
    fw = w_down.shape[1]
    me, mine = lax.axis_index("dp"), lax.axis_index("expert")

    code = (expert_ids + EXPERTS * dropped).astype(F32)
    info = jnp.concatenate([code.T, probs.astype(F32).T], axis=0)
    info = lax.all_gather(info, ("dp", "expert"), axis=0, tiled=False)
    info = info.reshape(n_dp, n_ex, 2 * top, rows)

    def spread(x):
        pieces = [
            lax.dynamic_slice_in_dim(x, (me ^ r) * part, part, axis=1) for r in range(n_dp)
        ]
        got = jnp.stack(swap_rel(pieces, "dp"), axis=0)
        return lax.all_gather(got, "expert", axis=0, tiled=False)

    og = spread(out_grad)
    tk = spread(tokens)
    pre = gather_rel(preacts[0], "dp").reshape(n_dp, local, n_ex, CAP, 2 * fw)

    info = jnp.stack([info[me ^ r] for r in range(n_dp)], axis=1)
    code_all, prob_all = info[:, :, :top], info[:, :, top:]
    experts = (mine * local + jnp.arange(local)).astype(F32)[:, None, None]
    kept_k = (code_all[:, :, None] == experts).astype(F32)
    drop_k = (code_all[:, :, None] == experts + EXPERTS).astype(F32)
    kept = jnp.sum(kept_k, axis=3)
    here = kept + jnp.sum(drop_k, axis=3)
    prob_t = jnp.sum(kept_k * prob_all[:, :, None], axis=3)
    earlier = (jnp.arange(rows)[:, None] < jnp.arange(rows)[None, :]).astype(BF)
    pos = jnp.dot(
        here.astype(BF).reshape(-1, rows), earlier, preferred_element_type=F32
    ).reshape(here.shape)
    pos = jnp.where(kept > 0, pos, -1.0)
    hot = pos[:, :, :, None, :] == jnp.arange(CAP, dtype=F32)[:, None]
    ps = jnp.sum(jnp.where(hot, prob_t[:, :, :, None, :], 0.0), axis=-1)
    ps = jnp.transpose(ps, (1, 2, 0, 3))[..., None]
    pick = hot.astype(BF)

    gs = jnp.einsum("jreqt,jrtd->erjqd", pick, og, preferred_element_type=F32).astype(BF)
    proj = jnp.einsum("erjqd,efd->rejqf", gs, w_down, preferred_element_type=F32)
    own = scatter_rel(proj, "dp", BF)
    proj = gather_rel(own.astype(BF), "dp").astype(F32)

    gate, up = pre[..., :fw].astype(F32), pre[..., fw:].astype(F32)
    sig = jax.nn.sigmoid(gate)
    silu = gate * sig
    hidden = silu * up
    slot_prob = jnp.sum(hidden[0] * own, axis=-1).astype(BF).astype(F32)
    scaled = ps * proj
    dgu = jnp.concatenate(
        [scaled * up * sig * (1.0 + gate * (1.0 - sig)), scaled * silu], axis=-1
    ).astype(BF)
    hidden_p = (ps * hidden).astype(BF)

    slot_grad = jnp.einsum("rejqf,edf->erjqd", dgu, w_gu, preferred_element_type=F32).astype(BF)
    tok = jnp.einsum("jreqt,erjqd->jrtd", pick, slot_grad, preferred_element_type=F32).astype(BF)
    tok = lax.psum_scatter(tok, "expert", scatter_dimension=0, tiled=False)
    tok = swap_rel([tok[r] for r in range(n_dp)], "dp")
    tok = jnp.stack(tok, axis=0)
    tok_grad = jnp.concatenate([tok[me ^ p] for p in range(n_dp)], axis=-1)

    back = jnp.sum(
        jnp.where(hot[:, 0], jnp.transpose(slot_prob, (1, 0, 2))[..., None], 0.0), axis=2
    )
    back = lax.all_to_all(back, "expert", split_axis=0, concat_axis=0, tiled=True)
    back = back.reshape(EXPERTS, rows)
    named = code.T[:, None, :] == jnp.arange(EXPERTS, dtype=F32)[:, None]
    prob_grad = jnp.sum(jnp.where(named, back[None], 0.0), axis=1).T.astype(BF)

    xs = jnp.einsum("jreqt,jrtd->erjqd", pick, tk, preferred_element_type=F32).astype(BF)
    grad_down = jnp.einsum("rejqf,erjqd->efd", hidden_p, gs, preferred_element_type=F32)
    grad_gu = jnp.einsum("erjqd,rejqf->edf", xs, dgu, preferred_element_type=F32)
    square = jnp.sum(grad_gu * grad_gu) + jnp.sum(grad_down * grad_down)
    mean_square = lax.psum(square, ("dp", "expert")) / (EXPERTS * 3 * width * fw)
    return tok_grad, prob_grad, grad_gu, grad_down, mean_square


def solution(mesh):
    both = P(("dp", "expert"), None)
    weights = (P("expert", "dp", None), P("expert", None, "dp"))
    return jax.shard_map(
        body,
        mesh=mesh,
        in_specs=(both,) * 5 + (P("dp", "expert", None, None),) + weights,
        out_specs=(both, both) + weights + (P(),),
        check_vma=False,
    )
```

```python
import functools

import jax
import jax.numpy as jnp
from jax import lax
from jax.experimental import pallas as pl
from jax.experimental.pallas import tpu as pltpu
from jax.sharding import PartitionSpec as P

EXPERTS = 32
CAP = 40
BF = jnp.bfloat16
F32 = jnp.float32


def xor_permute(x, axis, bit):
    n = lax.axis_size(axis)
    return lax.ppermute(x, axis, [(a, a ^ bit) for a in range(n)])


def gather_rel(x, axis):
    n = lax.axis_size(axis)
    buf = x[None]
    bit = n // 2
    while bit:
        other = xor_permute(buf, axis, bit)
        buf = jnp.stack([buf, other], axis=1).reshape((-1,) + x.shape)
        bit //= 2
    return buf


def swap_rel(pieces, axis):
    return [pieces[0]] + [xor_permute(pieces[r], axis, r) for r in range(1, len(pieces))]


def remote(src, dst, sems, slot, axis, peer):
    return pltpu.make_async_remote_copy(
        src_ref=src,
        dst_ref=dst,
        send_sem=sems.at[(0,) + slot],
        recv_sem=sems.at[(1,) + slot],
        device_id={axis: peer},
        device_id_type=pl.DeviceIdType.MESH,
    )


def greet(n_ex, n_dp, with_dp):
    j = lax.axis_index("expert")
    lines = n_ex // 2
    z = j // 2
    barrier = pltpu.get_barrier_semaphore()

    def signal(axis, peer):
        pl.semaphore_signal(
            barrier, inc=1, device_id={axis: peer}, device_id_type=pl.DeviceIdType.MESH
        )

    count = 1
    signal("expert", z * 2 + 1 - j % 2)

    @pl.when(z > 0)
    def _():
        signal("expert", j - 2)

    @pl.when(z < lines - 1)
    def _():
        signal("expert", j + 2)

    if with_dp:
        me = lax.axis_index("dp")
        bit = 1
        while bit < n_dp:
            signal("dp", flip(me, bit))
            count += 1
            bit *= 2
    count += (z + lines - 1) // lines + (2 * lines - 2 - z) // lines
    pl.semaphore_wait(barrier, count)


def flip(me, bit):
    return me + bit - 2 * bit * ((me // bit) % 2)


def expert_gather(n_ex, pairs, sems, local_sems):
    j = lax.axis_index("expert")
    lines = n_ex // 2
    z, x = j // 2, j % 2
    partner = z * 2 + 1 - x
    todo = []

    def up(a, s):
        i, o = pairs[a]
        b = (z - s) * 2 + x
        return remote(i if s == 0 else o.at[b], o.at[b], sems, (a, 0, s), "expert", j + 2)

    def down(a, s):
        i, o = pairs[a]
        b = (z + s) * 2 + x
        return remote(i if s == 0 else o.at[b], o.at[b], sems, (a, 1, s), "expert", j - 2)

    def across(a, z_of, first, s, side):
        i, o = pairs[a]
        b = z_of * 2 + x
        return remote(i if first else o.at[b], o.at[b], sems, (a, 2 + side, s), "expert", partner)

    def landed(a, b, kind, s):
        i, o = pairs[a]
        return remote(i, o.at[b], sems, (a, kind, s), "expert", partner)

    def begin():
        for a, (i, o) in enumerate(pairs):
            pltpu.make_async_copy(i, o.at[j], local_sems.at[a]).start()

            @pl.when(z < lines - 1)
            def _():
                up(a, 0).start()

            @pl.when(z > 0)
            def _():
                down(a, 0).start()

            across(a, z, True, 0, 0).start()

    def step(s):
        for a in range(len(pairs)):

            @pl.when(z - 1 - s >= 0)
            def _():
                landed(a, (z - 1 - s) * 2 + x, 0, s).wait_recv()
                if s + 1 < lines - 1:

                    @pl.when(z < lines - 1)
                    def _():
                        up(a, s + 1).start()

                across(a, z - 1 - s, False, s + 1, 0).start()

            @pl.when(z + 1 + s < lines)
            def _():
                landed(a, (z + 1 + s) * 2 + x, 1, s).wait_recv()
                if s + 1 < lines - 1:

                    @pl.when(z > 0)
                    def _():
                        down(a, s + 1).start()

                across(a, z + 1 + s, False, s + 1, 1).start()

    def finish():
        for a, (i, o) in enumerate(pairs):
            pltpu.make_async_copy(i, o.at[j], local_sems.at[a]).wait()
            landed(a, partner, 2, 0).wait_recv()
            across(a, z, True, 0, 0).wait_send()
            for s in range(lines - 1):

                @pl.when((z - s >= 0) & (z < lines - 1))
                def _():
                    up(a, s).wait_send()

                @pl.when((z + s < lines) & (z > 0))
                def _():
                    down(a, s).wait_send()

                @pl.when(z - 1 - s >= 0)
                def _():
                    across(a, z - 1 - s, False, s + 1, 0).wait_send()
                    landed(a, (z - 1 - s) * 2 + 1 - x, 2, s + 1).wait_recv()

                @pl.when(z + 1 + s < lines)
                def _():
                    across(a, z + 1 + s, False, s + 1, 1).wait_send()
                    landed(a, (z + 1 + s) * 2 + 1 - x, 3, s + 1).wait_recv()

    todo.append(begin)
    for s in range(lines - 1):
        todo.append(functools.partial(step, s))
    todo.append(finish)
    return todo


def dp_gather(n_dp, own, out, sems, chunks):
    me = lax.axis_index("dp")
    bits = []
    bit = n_dp // 2
    while bit:
        bits.append(bit)
        bit //= 2
    size = out.shape[1] // chunks

    def copy(level, r, c):
        rows = pl.ds(c * size, size)
        src = own.at[rows] if r == 0 else out.at[r, rows]
        bit = bits[level]
        return remote(src, out.at[r + bit, rows], sems, (level, r // (2 * bit), c), "dp", flip(me, bit))

    def held(level):
        return range(0, n_dp, 2 * bits[level])

    def send(level, c):
        if level:
            for r in held(level - 1):
                copy(level - 1, r, c).wait_recv()
        for r in held(level):
            copy(level, r, c).start()

    def finish():
        for c in range(chunks):
            for r in held(len(bits) - 1):
                copy(len(bits) - 1, r, c).wait_recv()
            for level in range(len(bits)):
                for r in held(level):
                    copy(level, r, c).wait_send()

    return send, finish, len(bits)


def first_kernel(n_ex, n_dp, og, info, pre, og_all, info_all, pre_all, sems, local_sems, dp_sems, dp_local):
    greet(n_ex, n_dp, True)
    todo = expert_gather(n_ex, [(info, info_all), (og, og_all)], sems, local_sems)
    send, finish, levels = dp_gather(n_dp, pre, pre_all, dp_sems, 2)
    keep = pltpu.make_async_copy(pre, pre_all.at[0], dp_local)
    todo[0]()
    for c in range(2):
        send(0, c)
    keep.start()
    todo[1]()
    for t in todo[2:-1]:
        t()
    for level in range(1, levels):
        for c in range(2):
            send(level, c)
    todo[-1]()
    finish()
    keep.wait()


def second_kernel(n_ex, n_dp, chunks, tk, part, tk_all, own_out, proj_all, *scratch):
    sems, local_sems, dp_sems, sum_sems = scratch[:4]
    scratch = scratch[4:]
    levels = len(scratch) // 2
    got, acc = scratch[:levels], (part,) + scratch[levels:]
    me = lax.axis_index("dp")
    size = own_out.shape[0] // chunks
    greet(n_ex, n_dp, True)
    todo = expert_gather(n_ex, [(tk, tk_all)], sems, local_sems)
    send, finish, gather_levels = dp_gather(n_dp, proj_all.at[0], proj_all, dp_sems, chunks)

    def copy(level, k, c):
        rows = pl.ds(c * size, size)
        return remote(
            acc[level].at[2 * k + 1, rows], got[level].at[k, rows], sums(level), (k, c), "dp", flip(me, 1 << level)
        )

    def sums(level):
        return sum_sems.at[level]

    def count(level):
        return n_dp >> (level + 1)

    def reduce(level, c):
        rows = pl.ds(c * size, size)
        for k in range(count(level)):
            copy(level, k, c).wait_recv()
            total = acc[level][2 * k, rows, :].astype(F32) + got[level][k, rows, :].astype(F32)
            if level + 1 < levels:
                acc[level + 1][k, rows, :] = total.astype(BF)
            else:
                own_out[rows, :] = total
                proj_all[0, rows, :] = total.astype(BF)
        if level + 1 < levels:
            for k in range(count(level + 1)):
                copy(level + 1, k, c).start()
        else:
            send(0, c)

    for c in range(chunks):
        for k in range(count(0)):
            copy(0, k, c).start()
    todo[0]()
    rest = list(todo[1:-1])
    for level in range(levels):
        for c in range(chunks):
            reduce(level, c)
            if level == levels - 1 and c % 2 and rest:
                rest.pop(0)()
    for level in range(1, gather_levels):
        for c in range(chunks):
            send(level, c)
            if rest:
                rest.pop(0)()
    for t in rest:
        t()
    todo[-1]()
    finish()
    for level in range(levels):
        for k in range(count(level)):
            for c in range(chunks):
                copy(level, k, c).wait_send()


ANY = pl.BlockSpec(memory_space=pl.ANY)
VM = pl.BlockSpec(memory_space=pltpu.VMEM)


def gather_first(n_ex, n_dp, og, info, pre):
    dma = pltpu.SemaphoreType.DMA
    lines, bits = n_ex // 2, n_dp.bit_length() - 1
    return pl.pallas_call(
        functools.partial(first_kernel, n_ex, n_dp),
        out_shape=(
            jax.ShapeDtypeStruct((n_ex,) + og.shape, og.dtype),
            jax.ShapeDtypeStruct((n_ex,) + info.shape, info.dtype),
            jax.ShapeDtypeStruct((n_dp,) + pre.shape, pre.dtype),
        ),
        in_specs=[ANY] * 3,
        out_specs=[ANY] * 3,
        scratch_shapes=[
            dma((2, 2, 4, lines)),
            dma((2,)),
            dma((2, bits, n_dp // 2, 2)),
            dma,
        ],
        compiler_params=pltpu.CompilerParams(
            collective_id=0, has_side_effects=True, vmem_limit_bytes=48 << 20
        ),
    )(og, info, pre)


def gather_second(n_ex, n_dp, tk, part):
    dma = pltpu.SemaphoreType.DMA
    lines, bits = n_ex // 2, n_dp.bit_length() - 1
    rows, cols = part.shape[1:]
    chunks = 4
    half = [pltpu.VMEM((n_dp >> (b + 1), rows, cols), BF) for b in range(bits)]
    return pl.pallas_call(
        functools.partial(second_kernel, n_ex, n_dp, chunks),
        out_shape=(
            jax.ShapeDtypeStruct((n_ex,) + tk.shape, tk.dtype),
            jax.ShapeDtypeStruct((rows, cols), F32),
            jax.ShapeDtypeStruct((n_dp, rows, cols), BF),
        ),
        in_specs=[ANY, VM],
        out_specs=[ANY, VM, VM],
        scratch_shapes=[
            dma((2, 1, 4, lines)),
            dma((1,)),
            dma((2, bits, n_dp // 2, chunks)),
            dma((bits, 2, n_dp // 2, chunks)),
        ]
        + half
        + half,
        compiler_params=pltpu.CompilerParams(
            collective_id=1, has_side_effects=True, vmem_limit_bytes=48 << 20
        ),
    )(tk, part)


def body(tokens, out_grad, probs, expert_ids, dropped, preacts, w_gu, w_down):
    n_dp, n_ex = lax.axis_size("dp"), lax.axis_size("expert")
    local = EXPERTS // n_ex
    rows, width = tokens.shape
    top = probs.shape[1]
    part = width // n_dp
    fw = w_down.shape[1]
    me, mine = lax.axis_index("dp"), lax.axis_index("expert")

    code = (expert_ids + EXPERTS * dropped).astype(F32)
    info = jnp.concatenate([code.T, probs.astype(F32).T], axis=0)
    info = gather_rel(info, "dp")

    def spread(x):
        pieces = [
            lax.dynamic_slice_in_dim(x, (me ^ r) * part, part, axis=1) for r in range(n_dp)
        ]
        return jnp.stack(swap_rel(pieces, "dp"), axis=0)

    og = spread(out_grad)
    tk = spread(tokens)
    og, info, pre = gather_first(n_ex, n_dp, og, info, preacts.reshape(-1, 2 * fw))
    pre = pre.reshape(n_dp, local, n_ex, CAP, 2 * fw)
    code_all, prob_all = info[:, :, :top], info[:, :, top:]
    experts = (mine * local + jnp.arange(local)).astype(F32)[:, None, None]
    kept_k = (code_all[:, :, None] == experts).astype(F32)
    drop_k = (code_all[:, :, None] == experts + EXPERTS).astype(F32)
    kept = jnp.sum(kept_k, axis=3)
    here = kept + jnp.sum(drop_k, axis=3)
    prob_t = jnp.sum(kept_k * prob_all[:, :, None], axis=3)
    earlier = (jnp.arange(rows)[:, None] < jnp.arange(rows)[None, :]).astype(BF)
    pos = jnp.dot(
        here.astype(BF).reshape(-1, rows), earlier, preferred_element_type=F32
    ).reshape(here.shape)
    pos = jnp.where(kept > 0, pos, -1.0)
    hot = pos[:, :, :, None, :] == jnp.arange(CAP, dtype=F32)[:, None]
    ps = jnp.sum(jnp.where(hot, prob_t[:, :, :, None, :], 0.0), axis=-1)
    ps = jnp.transpose(ps, (1, 2, 0, 3))[..., None]
    pick = hot.astype(BF)

    gs = jnp.einsum("jreqt,jrtd->erjqd", pick, og, preferred_element_type=F32).astype(BF)
    proj = jnp.einsum("erjqd,efd->rejqf", gs, w_down, preferred_element_type=F32)
    proj = proj.astype(BF).reshape(n_dp, -1, fw)
    tk, own, proj = gather_second(n_ex, n_dp, tk, proj)
    own = own.reshape(local, n_ex, CAP, fw)
    proj = proj.reshape((n_dp,) + own.shape).astype(F32)

    gate, up = pre[..., :fw].astype(F32), pre[..., fw:].astype(F32)
    sig = jax.nn.sigmoid(gate)
    silu = gate * sig
    hidden = silu * up
    slot_prob = jnp.sum(hidden[0] * own, axis=-1).astype(BF).astype(F32)
    scaled = ps * proj
    dgu = jnp.concatenate(
        [scaled * up * sig * (1.0 + gate * (1.0 - sig)), scaled * silu], axis=-1
    ).astype(BF)
    hidden_p = (ps * hidden).astype(BF)

    slot_grad = jnp.einsum("rejqf,edf->erjqd", dgu, w_gu, preferred_element_type=F32).astype(BF)
    tok = jnp.einsum("jreqt,erjqd->jrtd", pick, slot_grad, preferred_element_type=F32).astype(BF)
    tok = lax.psum_scatter(tok, "expert", scatter_dimension=0, tiled=False)
    tok = swap_rel([tok[r] for r in range(n_dp)], "dp")
    tok = jnp.stack(tok, axis=0)
    tok_grad = jnp.concatenate([tok[me ^ p] for p in range(n_dp)], axis=-1)

    back = jnp.sum(
        jnp.where(hot[:, 0], jnp.transpose(slot_prob, (1, 0, 2))[..., None], 0.0), axis=2
    )
    back = lax.all_to_all(back, "expert", split_axis=0, concat_axis=0, tiled=True)
    back = back.reshape(EXPERTS, rows)
    named = code.T[:, None, :] == jnp.arange(EXPERTS, dtype=F32)[:, None]
    prob_grad = jnp.sum(jnp.where(named, back[None], 0.0), axis=1).T.astype(BF)

    xs = jnp.einsum("jreqt,jrtd->erjqd", pick, tk, preferred_element_type=F32).astype(BF)
    grad_down = jnp.einsum("rejqf,erjqd->efd", hidden_p, gs, preferred_element_type=F32)
    grad_gu = jnp.einsum("erjqd,rejqf->edf", xs, dgu, preferred_element_type=F32)
    square = jnp.sum(grad_gu * grad_gu) + jnp.sum(grad_down * grad_down)
    mean_square = lax.psum(square, ("dp", "expert")) / (EXPERTS * 3 * width * fw)
    return tok_grad, prob_grad, grad_gu, grad_down, mean_square


def solution(mesh):
    both = P(("dp", "expert"), None)
    weights = (P("expert", "dp", None), P("expert", None, "dp"))
    return jax.shard_map(
        body,
        mesh=mesh,
        in_specs=(both,) * 5 + (P("dp", "expert", None, None),) + weights,
        out_specs=(both, both) + weights + (P(),),
        check_vma=False,
    )
```

```python
import functools

import jax
import jax.numpy as jnp
from jax import lax
from jax.experimental import pallas as pl
from jax.experimental.pallas import tpu as pltpu
from jax.sharding import PartitionSpec as P

EXPERTS = 32
CAP = 40
BF = jnp.bfloat16
F32 = jnp.float32


def xor_permute(x, axis, bit):
    n = lax.axis_size(axis)
    return lax.ppermute(x, axis, [(a, a ^ bit) for a in range(n)])


def gather_rel(x, axis):
    n = lax.axis_size(axis)
    buf = x[None]
    bit = n // 2
    while bit:
        other = xor_permute(buf, axis, bit)
        buf = jnp.stack([buf, other], axis=1).reshape((-1,) + x.shape)
        bit //= 2
    return buf


def swap_rel(pieces, axis):
    return [pieces[0]] + [xor_permute(pieces[r], axis, r) for r in range(1, len(pieces))]


def remote(src, dst, sems, slot, axis, peer):
    return pltpu.make_async_remote_copy(
        src_ref=src,
        dst_ref=dst,
        send_sem=sems.at[(0,) + slot],
        recv_sem=sems.at[(1,) + slot],
        device_id={axis: peer},
        device_id_type=pl.DeviceIdType.MESH,
    )


def greet(n_ex, n_dp, with_dp):
    j = lax.axis_index("expert")
    lines = n_ex // 2
    z = j // 2
    barrier = pltpu.get_barrier_semaphore()

    def signal(axis, peer):
        pl.semaphore_signal(
            barrier, inc=1, device_id={axis: peer}, device_id_type=pl.DeviceIdType.MESH
        )

    count = 1
    signal("expert", z * 2 + 1 - j % 2)

    @pl.when(z > 0)
    def _():
        signal("expert", j - 2)

    @pl.when(z < lines - 1)
    def _():
        signal("expert", j + 2)

    if with_dp:
        me = lax.axis_index("dp")
        bit = 1
        while bit < n_dp:
            signal("dp", flip(me, bit))
            count += 1
            bit *= 2
    count += (z + lines - 1) // lines + (2 * lines - 2 - z) // lines
    pl.semaphore_wait(barrier, count)


def flip(me, bit):
    return me + bit - 2 * bit * ((me // bit) % 2)


def expert_gather(n_ex, pairs, sems, local_sems):
    j = lax.axis_index("expert")
    lines = n_ex // 2
    z, x = j // 2, j % 2
    partner = z * 2 + 1 - x
    todo = []

    def up(a, s):
        i, o = pairs[a]
        b = (z - s) * 2 + x
        return remote(i if s == 0 else o.at[b], o.at[b], sems, (a, 0, s), "expert", j + 2)

    def down(a, s):
        i, o = pairs[a]
        b = (z + s) * 2 + x
        return remote(i if s == 0 else o.at[b], o.at[b], sems, (a, 1, s), "expert", j - 2)

    def across(a, z_of, first, s, side):
        i, o = pairs[a]
        b = z_of * 2 + x
        return remote(i if first else o.at[b], o.at[b], sems, (a, 2 + side, s), "expert", partner)

    def landed(a, b, kind, s):
        i, o = pairs[a]
        return remote(i, o.at[b], sems, (a, kind, s), "expert", partner)

    def begin():
        for a, (i, o) in enumerate(pairs):
            pltpu.make_async_copy(i, o.at[j], local_sems.at[a]).start()

            @pl.when(z < lines - 1)
            def _():
                up(a, 0).start()

            @pl.when(z > 0)
            def _():
                down(a, 0).start()

            across(a, z, True, 0, 0).start()

    def step(s):
        for a in range(len(pairs)):

            @pl.when(z - 1 - s >= 0)
            def _():
                landed(a, (z - 1 - s) * 2 + x, 0, s).wait_recv()
                if s + 1 < lines - 1:

                    @pl.when(z < lines - 1)
                    def _():
                        up(a, s + 1).start()

                across(a, z - 1 - s, False, s + 1, 0).start()

            @pl.when(z + 1 + s < lines)
            def _():
                landed(a, (z + 1 + s) * 2 + x, 1, s).wait_recv()
                if s + 1 < lines - 1:

                    @pl.when(z > 0)
                    def _():
                        down(a, s + 1).start()

                across(a, z + 1 + s, False, s + 1, 1).start()

    def finish():
        for a, (i, o) in enumerate(pairs):
            pltpu.make_async_copy(i, o.at[j], local_sems.at[a]).wait()
            landed(a, partner, 2, 0).wait_recv()
            across(a, z, True, 0, 0).wait_send()
            for s in range(lines - 1):

                @pl.when((z - s >= 0) & (z < lines - 1))
                def _():
                    up(a, s).wait_send()

                @pl.when((z + s < lines) & (z > 0))
                def _():
                    down(a, s).wait_send()

                @pl.when(z - 1 - s >= 0)
                def _():
                    across(a, z - 1 - s, False, s + 1, 0).wait_send()
                    landed(a, (z - 1 - s) * 2 + 1 - x, 2, s + 1).wait_recv()

                @pl.when(z + 1 + s < lines)
                def _():
                    across(a, z + 1 + s, False, s + 1, 1).wait_send()
                    landed(a, (z + 1 + s) * 2 + 1 - x, 3, s + 1).wait_recv()

    todo.append(begin)
    for s in range(lines - 1):
        todo.append(functools.partial(step, s))
    todo.append(finish)
    return todo


def dp_gather(n_dp, own, out, sems, chunks):
    me = lax.axis_index("dp")
    bits = []
    bit = n_dp // 2
    while bit:
        bits.append(bit)
        bit //= 2
    size = out.shape[1] // chunks

    def copy(level, r, c):
        rows = pl.ds(c * size, size)
        src = own.at[rows] if r == 0 else out.at[r, rows]
        bit = bits[level]
        return remote(src, out.at[r + bit, rows], sems, (level, r // (2 * bit), c), "dp", flip(me, bit))

    def held(level):
        return range(0, n_dp, 2 * bits[level])

    def send(level, c):
        if level:
            for r in held(level - 1):
                copy(level - 1, r, c).wait_recv()
        for r in held(level):
            copy(level, r, c).start()

    def finish():
        for c in range(chunks):
            for r in held(len(bits) - 1):
                copy(len(bits) - 1, r, c).wait_recv()
            for level in range(len(bits)):
                for r in held(level):
                    copy(level, r, c).wait_send()

    return send, finish, len(bits)


def first_kernel(n_ex, n_dp, og, info, pre, og_all, info_all, pre_all, sems, local_sems, dp_sems, dp_local):
    greet(n_ex, n_dp, True)
    todo = expert_gather(n_ex, [(info, info_all), (og, og_all)], sems, local_sems)
    send, finish, levels = dp_gather(n_dp, pre, pre_all, dp_sems, 2)
    keep = pltpu.make_async_copy(pre, pre_all.at[0], dp_local)
    todo[0]()
    for c in range(2):
        send(0, c)
    keep.start()
    todo[1]()
    for t in todo[2:-1]:
        t()
    for level in range(1, levels):
        for c in range(2):
            send(level, c)
    todo[-1]()
    finish()
    keep.wait()


def second_kernel(n_ex, n_dp, chunks, tk, part, tk_all, own_out, proj_all, *scratch):
    sems, local_sems, dp_sems, sum_sems = scratch[:4]
    scratch = scratch[4:]
    levels = len(scratch) // 2
    got, acc = scratch[:levels], (part,) + scratch[levels:]
    me = lax.axis_index("dp")
    size = own_out.shape[0] // chunks
    greet(n_ex, n_dp, True)
    todo = expert_gather(n_ex, [(tk, tk_all)], sems, local_sems)
    send, finish, gather_levels = dp_gather(n_dp, proj_all.at[0], proj_all, dp_sems, chunks)

    def copy(level, k, c):
        rows = pl.ds(c * size, size)
        return remote(
            acc[level].at[2 * k + 1, rows], got[level].at[k, rows], sums(level), (k, c), "dp", flip(me, 1 << level)
        )

    def sums(level):
        return sum_sems.at[level]

    def count(level):
        return n_dp >> (level + 1)

    def reduce(level, c):
        rows = pl.ds(c * size, size)
        for k in range(count(level)):
            copy(level, k, c).wait_recv()
            total = acc[level][2 * k, rows, :].astype(F32) + got[level][k, rows, :].astype(F32)
            if level + 1 < levels:
                acc[level + 1][k, rows, :] = total.astype(BF)
            else:
                own_out[rows, :] = total
                proj_all[0, rows, :] = total.astype(BF)
        if level + 1 < levels:
            for k in range(count(level + 1)):
                copy(level + 1, k, c).start()
        else:
            send(0, c)

    for c in range(chunks):
        for k in range(count(0)):
            copy(0, k, c).start()
    todo[0]()
    rest = list(todo[1:-1])
    for level in range(levels):
        for c in range(chunks):
            reduce(level, c)
            if level == levels - 1 and c % 2 and rest:
                rest.pop(0)()
    for level in range(1, gather_levels):
        for c in range(chunks):
            send(level, c)
            if rest:
                rest.pop(0)()
    for t in rest:
        t()
    todo[-1]()
    finish()
    for level in range(levels):
        for k in range(count(level)):
            for c in range(chunks):
                copy(level, k, c).wait_send()


ANY = pl.BlockSpec(memory_space=pl.ANY)
VM = pl.BlockSpec(memory_space=pltpu.VMEM)


def gather_first(n_ex, n_dp, og, info, pre):
    dma = pltpu.SemaphoreType.DMA
    lines, bits = n_ex // 2, n_dp.bit_length() - 1
    return pl.pallas_call(
        functools.partial(first_kernel, n_ex, n_dp),
        out_shape=(
            jax.ShapeDtypeStruct((n_ex,) + og.shape, og.dtype),
            jax.ShapeDtypeStruct((n_ex,) + info.shape, info.dtype),
            jax.ShapeDtypeStruct((n_dp,) + pre.shape, pre.dtype),
        ),
        in_specs=[ANY] * 3,
        out_specs=[ANY] * 3,
        scratch_shapes=[
            dma((2, 2, 4, lines)),
            dma((2,)),
            dma((2, bits, n_dp // 2, 2)),
            dma,
        ],
        compiler_params=pltpu.CompilerParams(
            collective_id=0, has_side_effects=True, vmem_limit_bytes=48 << 20
        ),
    )(og, info, pre)


def gather_second(n_ex, n_dp, tk, part):
    dma = pltpu.SemaphoreType.DMA
    lines, bits = n_ex // 2, n_dp.bit_length() - 1
    rows, cols = part.shape[1:]
    chunks = 4
    half = [pltpu.VMEM((n_dp >> (b + 1), rows, cols), BF) for b in range(bits)]
    return pl.pallas_call(
        functools.partial(second_kernel, n_ex, n_dp, chunks),
        out_shape=(
            jax.ShapeDtypeStruct((n_ex,) + tk.shape, tk.dtype),
            jax.ShapeDtypeStruct((rows, cols), F32),
            jax.ShapeDtypeStruct((n_dp, rows, cols), BF),
        ),
        in_specs=[ANY, VM],
        out_specs=[ANY, VM, VM],
        scratch_shapes=[
            dma((2, 1, 4, lines)),
            dma((1,)),
            dma((2, bits, n_dp // 2, chunks)),
            dma((bits, 2, n_dp // 2, chunks)),
        ]
        + half
        + half,
        compiler_params=pltpu.CompilerParams(
            collective_id=1, has_side_effects=True, vmem_limit_bytes=48 << 20
        ),
    )(tk, part)


def mixed(me, r):
    bit = 1
    while bit <= r:
        if r & bit:
            me = flip(me, bit)
        bit *= 2
    return me


def third_kernel(n_ex, n_dp, tok, square, out, total_out, got, below, above, fin, box, tile, x_sems, line_sems, dp_sems, sum_sems, all_sems):
    j, me = lax.axis_index("expert"), lax.axis_index("dp")
    lines = n_ex // 2
    z, x = j // 2, j % 2
    partner = z * 2 + 1 - x
    barrier = pltpu.get_barrier_semaphore()
    for k in range(1, n_ex):
        pl.semaphore_signal(
            barrier, inc=1, device_id={"expert": (j + k) % n_ex}, device_id_type=pl.DeviceIdType.MESH
        )
    for r in range(1, n_dp):
        pl.semaphore_signal(
            barrier, inc=1, device_id={"dp": mixed(me, r)}, device_id_type=pl.DeviceIdType.MESH
        )
    pl.semaphore_wait(barrier, n_ex - 1 + n_dp - 1)

    def pair(side, d):
        there = z + d if side == 0 else z - d
        return remote(tok.at[there * 2 + 1 - x], got.at[there], x_sems, (side, d), "expert", partner)

    def on_line(side, d):
        return z + d < lines if side == 0 else z - d >= 0

    for d in range(lines - 1, 0, -1):
        for side in (0, 1):

            @pl.when(on_line(side, d))
            def _():
                pair(side, d).start()

    pair(0, 0).start()

    levels = n_dp.bit_length() - 1

    def swap_sum(level):
        return remote(tile.at[level], box.at[n_ex + level], sum_sems, (level,), "dp", flip(me, 1 << level))

    def hand(k):
        return remote(tile.at[levels], box.at[j], all_sems, (k,), "expert", (j + k) % n_ex)

    def handed(k):
        return remote(tile.at[levels], box.at[(j - k + n_ex) % n_ex], all_sems, (k,), "expert", (j + k) % n_ex)

    tile[0] = square[...]
    for level in range(levels):
        swap_sum(level).start()
        swap_sum(level).wait()
        tile[level + 1] = tile[level] + box[n_ex + level]
    for k in range(1, n_ex):
        hand(k).start()
    box[j] = tile[levels]

    def pass_on(side, d):
        there = z + d if side == 0 else z - d
        dst = below if side == 0 else above
        return remote(
            got.at[there], dst.at[d - 1], line_sems, (side, d - 1), "expert", j + 2 if side == 0 else j - 2
        )

    def arrived(side, d):
        dst = below if side == 0 else above
        return remote(tok.at[0], dst.at[d], line_sems, (side, d), "expert", partner)

    def landed(side, d):
        there = z + d if side == 0 else z - d
        return remote(tok.at[0], got.at[there], x_sems, (side, d), "expert", partner)

    for d in range(lines - 1, 0, -1):
        for side in (0, 1):

            @pl.when(on_line(side, d))
            def _():
                there = z + d if side == 0 else z - d
                landed(side, d).wait_recv()
                got[there] = (tok[there * 2 + x].astype(F32) + got[there].astype(F32)).astype(BF)
                if d <= lines - 2:

                    @pl.when((z > 0) if side == 0 else (z < lines - 1))
                    def _():
                        arrived(side, d).wait_recv()
                        more = below[d] if side == 0 else above[d]
                        got[there] = (got[there].astype(F32) + more.astype(F32)).astype(BF)

                pass_on(side, d).start()

    landed(0, 0).wait_recv()
    fin[...] = tok[j].astype(F32) + got[z].astype(F32)

    @pl.when(z > 0)
    def _():
        arrived(0, 0).wait_recv()
        fin[...] += below[0].astype(F32)

    @pl.when(z < lines - 1)
    def _():
        arrived(1, 0).wait_recv()
        fin[...] += above[0].astype(F32)

    got[z] = fin[...].astype(BF)

    def slice_to(r):
        return remote(got.at[z, r], out.at[me], dp_sems, (r,), "dp", mixed(me, r))

    def slice_from(r):
        return remote(got.at[z, r], out.at[mixed(me, r)], dp_sems, (r,), "dp", mixed(me, r))

    for r in range(n_dp - 1, 0, -1):
        slice_to(r).start()
    out[me] = got[z, 0]
    for k in range(1, n_ex):
        handed(k).wait_recv()
        hand(k).wait_send()
    total = box[0]
    for k in range(1, n_ex):
        total = total + box[k]
    total_out[...] = total
    for r in range(1, n_dp):
        slice_from(r).wait_recv()
        slice_to(r).wait_send()
    pair(0, 0).wait_send()
    for d in range(1, lines):
        for side in (0, 1):

            @pl.when(on_line(side, d))
            def _():
                pair(side, d).wait_send()
                pass_on(side, d).wait_send()


def scatter_third(n_ex, n_dp, tok, square):
    dma = pltpu.SemaphoreType.DMA
    lines, bits = n_ex // 2, n_dp.bit_length() - 1
    block = tok.shape[1:]
    return pl.pallas_call(
        functools.partial(third_kernel, n_ex, n_dp),
        out_shape=(
            jax.ShapeDtypeStruct(block, BF),
            jax.ShapeDtypeStruct(square.shape, F32),
        ),
        in_specs=[VM] * 2,
        out_specs=[VM] * 2,
        scratch_shapes=[
            pltpu.VMEM((lines,) + block, BF),
            pltpu.VMEM((lines - 1,) + block, BF),
            pltpu.VMEM((lines - 1,) + block, BF),
            pltpu.VMEM(block, F32),
            pltpu.VMEM((n_ex + bits,) + square.shape, F32),
            pltpu.VMEM((bits + 1,) + square.shape, F32),
            dma((2, 2, lines)),
            dma((2, 2, lines)),
            dma((2, n_dp)),
            dma((2, bits)),
            dma((2, n_ex)),
        ],
        compiler_params=pltpu.CompilerParams(
            collective_id=2, has_side_effects=True, vmem_limit_bytes=56 << 20
        ),
    )(tok, square)


def body(tokens, out_grad, probs, expert_ids, dropped, preacts, w_gu, w_down):
    n_dp, n_ex = lax.axis_size("dp"), lax.axis_size("expert")
    local = EXPERTS // n_ex
    rows, width = tokens.shape
    top = probs.shape[1]
    part = width // n_dp
    fw = w_down.shape[1]
    me, mine = lax.axis_index("dp"), lax.axis_index("expert")

    code = (expert_ids + EXPERTS * dropped).astype(F32)
    info = jnp.concatenate([code.T, probs.astype(F32).T], axis=0)
    info = gather_rel(info, "dp")

    def spread(x):
        pieces = [
            lax.dynamic_slice_in_dim(x, (me ^ r) * part, part, axis=1) for r in range(n_dp)
        ]
        return jnp.stack(swap_rel(pieces, "dp"), axis=0)

    og = spread(out_grad)
    tk = spread(tokens)
    og, info, pre = gather_first(n_ex, n_dp, og, info, preacts.reshape(-1, 2 * fw))
    pre = pre.reshape(n_dp, local, n_ex, CAP, 2 * fw)
    code_all, prob_all = info[:, :, :top], info[:, :, top:]
    experts = (mine * local + jnp.arange(local)).astype(F32)[:, None, None]
    kept_k = (code_all[:, :, None] == experts).astype(F32)
    drop_k = (code_all[:, :, None] == experts + EXPERTS).astype(F32)
    kept = jnp.sum(kept_k, axis=3)
    here = kept + jnp.sum(drop_k, axis=3)
    prob_t = jnp.sum(kept_k * prob_all[:, :, None], axis=3)
    earlier = (jnp.arange(rows)[:, None] < jnp.arange(rows)[None, :]).astype(BF)
    pos = jnp.dot(
        here.astype(BF).reshape(-1, rows), earlier, preferred_element_type=F32
    ).reshape(here.shape)
    pos = jnp.where(kept > 0, pos, -1.0)
    hot = pos[:, :, :, None, :] == jnp.arange(CAP, dtype=F32)[:, None]
    ps = jnp.sum(jnp.where(hot, prob_t[:, :, :, None, :], 0.0), axis=-1)
    ps = jnp.transpose(ps, (1, 2, 0, 3))[..., None]
    pick = hot.astype(BF)

    gs = jnp.einsum("jreqt,jrtd->erjqd", pick, og, preferred_element_type=F32).astype(BF)
    proj = jnp.einsum("erjqd,efd->rejqf", gs, w_down, preferred_element_type=F32)
    proj = proj.astype(BF).reshape(n_dp, -1, fw)
    tk, own, proj = gather_second(n_ex, n_dp, tk, proj)
    own = own.reshape(local, n_ex, CAP, fw)
    proj = proj.reshape((n_dp,) + own.shape).astype(F32)

    gate, up = pre[..., :fw].astype(F32), pre[..., fw:].astype(F32)
    sig = jax.nn.sigmoid(gate)
    silu = gate * sig
    hidden = silu * up
    slot_prob = jnp.sum(hidden[0] * own, axis=-1).astype(BF).astype(F32)
    scaled = ps * proj
    dgu = jnp.concatenate(
        [scaled * up * sig * (1.0 + gate * (1.0 - sig)), scaled * silu], axis=-1
    ).astype(BF)
    hidden_p = (ps * hidden).astype(BF)

    slot_grad = jnp.einsum("rejqf,edf->erjqd", dgu, w_gu, preferred_element_type=F32).astype(BF)
    tok = jnp.einsum("jreqt,erjqd->jrtd", pick, slot_grad, preferred_element_type=F32).astype(BF)
    back = jnp.sum(
        jnp.where(hot[:, 0], jnp.transpose(slot_prob, (1, 0, 2))[..., None], 0.0), axis=2
    )
    back = lax.all_to_all(back, "expert", split_axis=0, concat_axis=0, tiled=True)
    back = back.reshape(EXPERTS, rows)
    named = code.T[:, None, :] == jnp.arange(EXPERTS, dtype=F32)[:, None]
    prob_grad = jnp.sum(jnp.where(named, back[None], 0.0), axis=1).T.astype(BF)

    xs = jnp.einsum("jreqt,jrtd->erjqd", pick, tk, preferred_element_type=F32).astype(BF)
    grad_down = jnp.einsum("rejqf,erjqd->efd", hidden_p, gs, preferred_element_type=F32)
    grad_gu = jnp.einsum("erjqd,rejqf->edf", xs, dgu, preferred_element_type=F32)
    square = jnp.sum(grad_gu * grad_gu) + jnp.sum(grad_down * grad_down)
    tok, total = scatter_third(n_ex, n_dp, tok, jnp.full((8, 128), square, F32))
    tok_grad = jnp.transpose(tok, (1, 0, 2)).reshape(rows, width)
    mean_square = total[0, 0] / (EXPERTS * 3 * width * fw)
    return tok_grad, prob_grad, grad_gu, grad_down, mean_square


def solution(mesh):
    both = P(("dp", "expert"), None)
    weights = (P("expert", "dp", None), P("expert", None, "dp"))
    return jax.shard_map(
        body,
        mesh=mesh,
        in_specs=(both,) * 5 + (P("dp", "expert", None, None),) + weights,
        out_specs=(both, both) + weights + (P(),),
        check_vma=False,
    )
```

```python
import functools

import jax
import jax.numpy as jnp
from jax import lax
from jax.experimental import pallas as pl
from jax.experimental.pallas import tpu as pltpu
from jax.sharding import PartitionSpec as P

EXPERTS = 32
CAP = 40
BF = jnp.bfloat16
F32 = jnp.float32


def xor_permute(x, axis, bit):
    n = lax.axis_size(axis)
    return lax.ppermute(x, axis, [(a, a ^ bit) for a in range(n)])


def gather_rel(x, axis):
    n = lax.axis_size(axis)
    buf = x[None]
    bit = n // 2
    while bit:
        other = xor_permute(buf, axis, bit)
        buf = jnp.stack([buf, other], axis=1).reshape((-1,) + x.shape)
        bit //= 2
    return buf


def swap_rel(pieces, axis):
    return [pieces[0]] + [xor_permute(pieces[r], axis, r) for r in range(1, len(pieces))]


def remote(src, dst, sems, slot, axis, peer):
    return pltpu.make_async_remote_copy(
        src_ref=src,
        dst_ref=dst,
        send_sem=sems.at[(0,) + slot],
        recv_sem=sems.at[(1,) + slot],
        device_id={axis: peer},
        device_id_type=pl.DeviceIdType.MESH,
    )


def greet(n_ex, n_dp, with_dp):
    j = lax.axis_index("expert")
    lines = n_ex // 2
    z = j // 2
    barrier = pltpu.get_barrier_semaphore()

    def signal(axis, peer):
        pl.semaphore_signal(
            barrier, inc=1, device_id={axis: peer}, device_id_type=pl.DeviceIdType.MESH
        )

    count = 1
    signal("expert", z * 2 + 1 - j % 2)

    @pl.when(z > 0)
    def _():
        signal("expert", j - 2)

    @pl.when(z < lines - 1)
    def _():
        signal("expert", j + 2)

    if with_dp:
        me = lax.axis_index("dp")
        bit = 1
        while bit < n_dp:
            signal("dp", flip(me, bit))
            count += 1
            bit *= 2
    count += (z + lines - 1) // lines + (2 * lines - 2 - z) // lines
    pl.semaphore_wait(barrier, count)


def flip(me, bit):
    return me + bit - 2 * bit * ((me // bit) % 2)


def expert_gather(n_ex, pairs, sems, local_sems):
    j = lax.axis_index("expert")
    lines = n_ex // 2
    z, x = j // 2, j % 2
    partner = z * 2 + 1 - x
    todo = []

    def up(a, s):
        i, o = pairs[a]
        b = (z - s) * 2 + x
        return remote(i if s == 0 else o.at[b], o.at[b], sems, (a, 0, s), "expert", j + 2)

    def down(a, s):
        i, o = pairs[a]
        b = (z + s) * 2 + x
        return remote(i if s == 0 else o.at[b], o.at[b], sems, (a, 1, s), "expert", j - 2)

    def across(a, z_of, first, s, side):
        i, o = pairs[a]
        b = z_of * 2 + x
        if first:
            return remote(i, o.at[b], sems, (a, 2 + side, s), "expert", partner)
        most = pl.ds(1, i.shape[0] - 1)
        return remote(o.at[b, most], o.at[b, most], sems, (a, 2 + side, s), "expert", partner)

    def crossed(a, b, side, s):
        i, o = pairs[a]
        most = pl.ds(1, i.shape[0] - 1)
        return remote(i.at[most], o.at[b, most], sems, (a, 2 + side, s), "expert", partner)

    def aside(a, side, s):
        i, o = pairs[a]
        b = (z - s if side == 0 else z + s) * 2 + 1 - x
        return remote(o.at[b, 0], o.at[b, 0], sems, (a, 4 + side, s), "expert", j + 2 if side == 0 else j - 2)

    def aside_landed(a, side, s):
        i, o = pairs[a]
        b = (z - 1 - s if side == 0 else z + 1 + s) * 2 + 1 - x
        return remote(i.at[0], o.at[b, 0], sems, (a, 4 + side, s), "expert", partner)

    def relay(s):
        for a in range(len(pairs)):
            if s < 0:
                landed(a, partner, 2, 0).wait_recv()

            for side in (0, 1):
                more = (z < lines - 1) if side == 0 else (z > 0)
                if s < 0:

                    @pl.when(more)
                    def _():
                        aside(a, side, 0).start()

                else:

                    @pl.when((z - 1 - s >= 0) if side == 0 else (z + 1 + s < lines))
                    def _():
                        aside_landed(a, side, s).wait_recv()
                        if s + 1 < lines - 1:

                            @pl.when(more)
                            def _():
                                aside(a, side, s + 1).start()

    def landed(a, b, kind, s):
        i, o = pairs[a]
        return remote(i, o.at[b], sems, (a, kind, s), "expert", partner)

    def begin():
        for a, (i, o) in enumerate(pairs):
            pltpu.make_async_copy(i, o.at[j], local_sems.at[a]).start()

            @pl.when(z < lines - 1)
            def _():
                up(a, 0).start()

            @pl.when(z > 0)
            def _():
                down(a, 0).start()

            across(a, z, True, 0, 0).start()

    def step(s):
        for a in range(len(pairs)):

            @pl.when(z - 1 - s >= 0)
            def _():
                landed(a, (z - 1 - s) * 2 + x, 0, s).wait_recv()
                if s + 1 < lines - 1:

                    @pl.when(z < lines - 1)
                    def _():
                        up(a, s + 1).start()

                across(a, z - 1 - s, False, s + 1, 0).start()

            @pl.when(z + 1 + s < lines)
            def _():
                landed(a, (z + 1 + s) * 2 + x, 1, s).wait_recv()
                if s + 1 < lines - 1:

                    @pl.when(z > 0)
                    def _():
                        down(a, s + 1).start()

                across(a, z + 1 + s, False, s + 1, 1).start()

    def finish():
        for a, (i, o) in enumerate(pairs):
            pltpu.make_async_copy(i, o.at[j], local_sems.at[a]).wait()
            across(a, z, True, 0, 0).wait_send()
            for s in range(lines - 1):

                @pl.when((z - s >= 0) & (z < lines - 1))
                def _():
                    aside(a, 0, s).wait_send()

                @pl.when((z + s < lines) & (z > 0))
                def _():
                    aside(a, 1, s).wait_send()

                @pl.when((z - s >= 0) & (z < lines - 1))
                def _():
                    up(a, s).wait_send()

                @pl.when((z + s < lines) & (z > 0))
                def _():
                    down(a, s).wait_send()

                @pl.when(z - 1 - s >= 0)
                def _():
                    across(a, z - 1 - s, False, s + 1, 0).wait_send()
                    crossed(a, (z - 1 - s) * 2 + 1 - x, 0, s + 1).wait_recv()

                @pl.when(z + 1 + s < lines)
                def _():
                    across(a, z + 1 + s, False, s + 1, 1).wait_send()
                    crossed(a, (z + 1 + s) * 2 + 1 - x, 1, s + 1).wait_recv()

    todo.append(begin)
    for s in range(lines - 1):
        todo.append(functools.partial(step, s))
        todo.append(functools.partial(relay, s - 1))
    todo.append(functools.partial(relay, lines - 2))
    todo.append(finish)
    return todo


def dp_gather(n_dp, own, out, sems, chunks):
    me = lax.axis_index("dp")
    bits = []
    bit = n_dp // 2
    while bit:
        bits.append(bit)
        bit //= 2
    size = out.shape[1] // chunks

    def copy(level, r, c):
        rows = pl.ds(c * size, size)
        src = own.at[rows] if r == 0 else out.at[r, rows]
        bit = bits[level]
        return remote(src, out.at[r + bit, rows], sems, (level, r // (2 * bit), c), "dp", flip(me, bit))

    def held(level):
        return range(0, n_dp, 2 * bits[level])

    def send(level, c):
        if level:
            for r in held(level - 1):
                copy(level - 1, r, c).wait_recv()
        for r in held(level):
            copy(level, r, c).start()

    def finish():
        for c in range(chunks):
            for r in held(len(bits) - 1):
                copy(len(bits) - 1, r, c).wait_recv()
            for level in range(len(bits)):
                for r in held(level):
                    copy(level, r, c).wait_send()

    return send, finish, len(bits)


def first_kernel(n_ex, n_dp, og, info, pre, og_all, info_all, pre_all, sems, local_sems, dp_sems, dp_local):
    greet(n_ex, n_dp, True)
    todo = expert_gather(n_ex, [(info, info_all), (og, og_all)], sems, local_sems)
    send, finish, levels = dp_gather(n_dp, pre, pre_all, dp_sems, 2)
    keep = pltpu.make_async_copy(pre, pre_all.at[0], dp_local)
    todo[0]()
    for c in range(2):
        send(0, c)
    keep.start()
    todo[1]()
    for t in todo[2:-1]:
        t()
    for level in range(1, levels):
        for c in range(2):
            send(level, c)
    todo[-1]()
    finish()
    keep.wait()


def second_kernel(n_ex, n_dp, chunks, tk, part, tk_all, own_out, proj_all, *scratch):
    sems, local_sems, dp_sems, sum_sems = scratch[:4]
    scratch = scratch[4:]
    levels = len(scratch) // 2
    got, acc = scratch[:levels], (part,) + scratch[levels:]
    me = lax.axis_index("dp")
    size = own_out.shape[0] // chunks
    greet(n_ex, n_dp, True)
    todo = expert_gather(n_ex, [(tk, tk_all)], sems, local_sems)
    send, finish, gather_levels = dp_gather(n_dp, proj_all.at[0], proj_all, dp_sems, chunks)

    def copy(level, k, c):
        rows = pl.ds(c * size, size)
        return remote(
            acc[level].at[2 * k + 1, rows], got[level].at[k, rows], sums(level), (k, c), "dp", flip(me, 1 << level)
        )

    def sums(level):
        return sum_sems.at[level]

    def count(level):
        return n_dp >> (level + 1)

    def reduce(level, c):
        rows = pl.ds(c * size, size)
        for k in range(count(level)):
            copy(level, k, c).wait_recv()
            total = acc[level][2 * k, rows, :].astype(F32) + got[level][k, rows, :].astype(F32)
            if level + 1 < levels:
                acc[level + 1][k, rows, :] = total.astype(BF)
            else:
                own_out[rows, :] = total
                proj_all[0, rows, :] = total.astype(BF)
        if level + 1 < levels:
            for k in range(count(level + 1)):
                copy(level + 1, k, c).start()
        else:
            send(0, c)

    for c in range(chunks):
        for k in range(count(0)):
            copy(0, k, c).start()
    todo[0]()
    rest = list(todo[1:-1])
    for level in range(levels):
        for c in range(chunks):
            reduce(level, c)
            if level == levels - 1 and c and rest:
                rest.pop(0)()
    for level in range(1, gather_levels):
        for c in range(chunks):
            send(level, c)
            if rest:
                rest.pop(0)()
    for t in rest:
        t()
    todo[-1]()
    finish()
    for level in range(levels):
        for k in range(count(level)):
            for c in range(chunks):
                copy(level, k, c).wait_send()


ANY = pl.BlockSpec(memory_space=pl.ANY)
VM = pl.BlockSpec(memory_space=pltpu.VMEM)


def gather_first(n_ex, n_dp, og, info, pre):
    dma = pltpu.SemaphoreType.DMA
    lines, bits = n_ex // 2, n_dp.bit_length() - 1
    return pl.pallas_call(
        functools.partial(first_kernel, n_ex, n_dp),
        out_shape=(
            jax.ShapeDtypeStruct((n_ex,) + og.shape, og.dtype),
            jax.ShapeDtypeStruct((n_ex,) + info.shape, info.dtype),
            jax.ShapeDtypeStruct((n_dp,) + pre.shape, pre.dtype),
        ),
        in_specs=[ANY] * 3,
        out_specs=[ANY] * 3,
        scratch_shapes=[
            dma((2, 2, 6, lines)),
            dma((2,)),
            dma((2, bits, n_dp // 2, 2)),
            dma,
        ],
        compiler_params=pltpu.CompilerParams(
            collective_id=0, has_side_effects=True, vmem_limit_bytes=48 << 20
        ),
    )(og, info, pre)


def gather_second(n_ex, n_dp, tk, part):
    dma = pltpu.SemaphoreType.DMA
    lines, bits = n_ex // 2, n_dp.bit_length() - 1
    rows, cols = part.shape[1:]
    chunks = 4
    half = [pltpu.VMEM((n_dp >> (b + 1), rows, cols), BF) for b in range(bits)]
    return pl.pallas_call(
        functools.partial(second_kernel, n_ex, n_dp, chunks),
        out_shape=(
            jax.ShapeDtypeStruct((n_ex,) + tk.shape, tk.dtype),
            jax.ShapeDtypeStruct((rows, cols), F32),
            jax.ShapeDtypeStruct((n_dp, rows, cols), BF),
        ),
        in_specs=[ANY, VM],
        out_specs=[ANY, VM, VM],
        scratch_shapes=[
            dma((2, 1, 6, lines)),
            dma((1,)),
            dma((2, bits, n_dp // 2, chunks)),
            dma((bits, 2, n_dp // 2, chunks)),
        ]
        + half
        + half,
        compiler_params=pltpu.CompilerParams(
            collective_id=1, has_side_effects=True, vmem_limit_bytes=48 << 20
        ),
    )(tk, part)


def mixed(me, r):
    bit = 1
    while bit <= r:
        if r & bit:
            me = flip(me, bit)
        bit *= 2
    return me


def third_kernel(n_ex, n_dp, tok, square, out, total_out, got, below, above, fin, box, tile, x_sems, line_sems, dp_sems, sum_sems, all_sems):
    j, me = lax.axis_index("expert"), lax.axis_index("dp")
    lines = n_ex // 2
    z, x = j // 2, j % 2
    partner = z * 2 + 1 - x
    barrier = pltpu.get_barrier_semaphore()
    for k in range(1, n_ex):
        pl.semaphore_signal(
            barrier, inc=1, device_id={"expert": (j + k) % n_ex}, device_id_type=pl.DeviceIdType.MESH
        )
    for r in range(1, n_dp):
        pl.semaphore_signal(
            barrier, inc=1, device_id={"dp": mixed(me, r)}, device_id_type=pl.DeviceIdType.MESH
        )
    pl.semaphore_wait(barrier, n_ex - 1 + n_dp - 1)

    def pair(side, d):
        there = z + d if side == 0 else z - d
        return remote(tok.at[there * 2 + 1 - x], got.at[there], x_sems, (side, d), "expert", partner)

    def on_line(side, d):
        return z + d < lines if side == 0 else z - d >= 0

    for d in range(lines - 1, 0, -1):
        for side in (0, 1):

            @pl.when(on_line(side, d))
            def _():
                pair(side, d).start()

    pair(0, 0).start()

    levels = n_dp.bit_length() - 1

    def swap_sum(level):
        return remote(tile.at[level], box.at[n_ex + level], sum_sems, (level,), "dp", flip(me, 1 << level))

    def hand(k):
        return remote(tile.at[levels], box.at[j], all_sems, (k,), "expert", (j + k) % n_ex)

    def handed(k):
        return remote(tile.at[levels], box.at[(j - k + n_ex) % n_ex], all_sems, (k,), "expert", (j + k) % n_ex)

    tile[0] = square[...]
    for level in range(levels):
        swap_sum(level).start()
        swap_sum(level).wait()
        tile[level + 1] = tile[level] + box[n_ex + level]
    for k in range(1, n_ex):
        hand(k).start()
    box[j] = tile[levels]

    def pass_on(side, d):
        there = z + d if side == 0 else z - d
        dst = below if side == 0 else above
        return remote(
            got.at[there], dst.at[d - 1], line_sems, (side, d - 1), "expert", j + 2 if side == 0 else j - 2
        )

    def arrived(side, d):
        dst = below if side == 0 else above
        return remote(tok.at[0], dst.at[d], line_sems, (side, d), "expert", partner)

    def landed(side, d):
        there = z + d if side == 0 else z - d
        return remote(tok.at[0], got.at[there], x_sems, (side, d), "expert", partner)

    for d in range(lines - 1, 0, -1):
        for side in (0, 1):

            @pl.when(on_line(side, d))
            def _():
                there = z + d if side == 0 else z - d
                landed(side, d).wait_recv()
                got[there] = (tok[there * 2 + x].astype(F32) + got[there].astype(F32)).astype(BF)
                if d <= lines - 2:

                    @pl.when((z > 0) if side == 0 else (z < lines - 1))
                    def _():
                        arrived(side, d).wait_recv()
                        more = below[d] if side == 0 else above[d]
                        got[there] = (got[there].astype(F32) + more.astype(F32)).astype(BF)

                pass_on(side, d).start()

    landed(0, 0).wait_recv()
    fin[...] = tok[j].astype(F32) + got[z].astype(F32)

    @pl.when(z > 0)
    def _():
        arrived(0, 0).wait_recv()
        fin[...] += below[0].astype(F32)

    @pl.when(z < lines - 1)
    def _():
        arrived(1, 0).wait_recv()
        fin[...] += above[0].astype(F32)

    got[z] = fin[...].astype(BF)

    def slice_to(r):
        return remote(got.at[z, r], out.at[me], dp_sems, (r,), "dp", mixed(me, r))

    def slice_from(r):
        return remote(got.at[z, r], out.at[mixed(me, r)], dp_sems, (r,), "dp", mixed(me, r))

    for r in range(n_dp - 1, 0, -1):
        slice_to(r).start()
    out[me] = got[z, 0]
    for k in range(1, n_ex):
        handed(k).wait_recv()
        hand(k).wait_send()
    total = box[0]
    for k in range(1, n_ex):
        total = total + box[k]
    total_out[...] = total
    for r in range(1, n_dp):
        slice_from(r).wait_recv()
        slice_to(r).wait_send()
    pair(0, 0).wait_send()
    for d in range(1, lines):
        for side in (0, 1):

            @pl.when(on_line(side, d))
            def _():
                pair(side, d).wait_send()
                pass_on(side, d).wait_send()


def scatter_third(n_ex, n_dp, tok, square):
    dma = pltpu.SemaphoreType.DMA
    lines, bits = n_ex // 2, n_dp.bit_length() - 1
    block = tok.shape[1:]
    return pl.pallas_call(
        functools.partial(third_kernel, n_ex, n_dp),
        out_shape=(
            jax.ShapeDtypeStruct(block, BF),
            jax.ShapeDtypeStruct(square.shape, F32),
        ),
        in_specs=[VM] * 2,
        out_specs=[VM] * 2,
        scratch_shapes=[
            pltpu.VMEM((lines,) + block, BF),
            pltpu.VMEM((lines - 1,) + block, BF),
            pltpu.VMEM((lines - 1,) + block, BF),
            pltpu.VMEM(block, F32),
            pltpu.VMEM((n_ex + bits,) + square.shape, F32),
            pltpu.VMEM((bits + 1,) + square.shape, F32),
            dma((2, 2, lines)),
            dma((2, 2, lines)),
            dma((2, n_dp)),
            dma((2, bits)),
            dma((2, n_ex)),
        ],
        compiler_params=pltpu.CompilerParams(
            collective_id=2, has_side_effects=True, vmem_limit_bytes=56 << 20
        ),
    )(tok, square)


def body(tokens, out_grad, probs, expert_ids, dropped, preacts, w_gu, w_down):
    n_dp, n_ex = lax.axis_size("dp"), lax.axis_size("expert")
    local = EXPERTS // n_ex
    rows, width = tokens.shape
    top = probs.shape[1]
    part = width // n_dp
    fw = w_down.shape[1]
    me, mine = lax.axis_index("dp"), lax.axis_index("expert")

    code = (expert_ids + EXPERTS * dropped).astype(F32)
    info = jnp.concatenate([code.T, probs.astype(F32).T], axis=0)
    info = gather_rel(info, "dp")

    def spread(x):
        pieces = [
            lax.dynamic_slice_in_dim(x, (me ^ r) * part, part, axis=1) for r in range(n_dp)
        ]
        return jnp.stack(swap_rel(pieces, "dp"), axis=0)

    og = spread(out_grad)
    tk = spread(tokens)
    og, info, pre = gather_first(n_ex, n_dp, og, info, preacts.reshape(-1, 2 * fw))
    pre = pre.reshape(n_dp, local, n_ex, CAP, 2 * fw)
    code_all, prob_all = info[:, :, :top], info[:, :, top:]
    experts = (mine * local + jnp.arange(local)).astype(F32)[:, None, None]
    kept_k = (code_all[:, :, None] == experts).astype(F32)
    drop_k = (code_all[:, :, None] == experts + EXPERTS).astype(F32)
    kept = jnp.sum(kept_k, axis=3)
    here = kept + jnp.sum(drop_k, axis=3)
    prob_t = jnp.sum(kept_k * prob_all[:, :, None], axis=3)
    earlier = (jnp.arange(rows)[:, None] < jnp.arange(rows)[None, :]).astype(BF)
    pos = jnp.dot(
        here.astype(BF).reshape(-1, rows), earlier, preferred_element_type=F32
    ).reshape(here.shape)
    pos = jnp.where(kept > 0, pos, -1.0)
    hot = pos[:, :, :, None, :] == jnp.arange(CAP, dtype=F32)[:, None]
    ps = jnp.sum(jnp.where(hot, prob_t[:, :, :, None, :], 0.0), axis=-1)
    ps = jnp.transpose(ps, (1, 2, 0, 3))[..., None]
    pick = hot.astype(BF)

    gs = jnp.einsum("jreqt,jrtd->erjqd", pick, og, preferred_element_type=F32).astype(BF)
    proj = jnp.einsum("erjqd,efd->rejqf", gs, w_down, preferred_element_type=F32)
    proj = proj.astype(BF).reshape(n_dp, -1, fw)
    tk, own, proj = gather_second(n_ex, n_dp, tk, proj)
    own = own.reshape(local, n_ex, CAP, fw)
    proj = proj.reshape((n_dp,) + own.shape).astype(F32)

    gate, up = pre[..., :fw].astype(F32), pre[..., fw:].astype(F32)
    sig = jax.nn.sigmoid(gate)
    silu = gate * sig
    hidden = silu * up
    slot_prob = jnp.sum(hidden[0] * own, axis=-1).astype(BF).astype(F32)
    scaled = ps * proj
    dgu = jnp.concatenate(
        [scaled * up * sig * (1.0 + gate * (1.0 - sig)), scaled * silu], axis=-1
    ).astype(BF)
    hidden_p = (ps * hidden).astype(BF)

    slot_grad = jnp.einsum("rejqf,edf->erjqd", dgu, w_gu, preferred_element_type=F32).astype(BF)
    tok = jnp.einsum("jreqt,erjqd->jrtd", pick, slot_grad, preferred_element_type=F32).astype(BF)
    back = jnp.sum(
        jnp.where(hot[:, 0], jnp.transpose(slot_prob, (1, 0, 2))[..., None], 0.0), axis=2
    )
    back = lax.all_to_all(back, "expert", split_axis=0, concat_axis=0, tiled=True)
    back = back.reshape(EXPERTS, rows)
    named = code.T[:, None, :] == jnp.arange(EXPERTS, dtype=F32)[:, None]
    prob_grad = jnp.sum(jnp.where(named, back[None], 0.0), axis=1).T.astype(BF)

    xs = jnp.einsum("jreqt,jrtd->erjqd", pick, tk, preferred_element_type=F32).astype(BF)
    grad_down = jnp.einsum("rejqf,erjqd->efd", hidden_p, gs, preferred_element_type=F32)
    grad_gu = jnp.einsum("erjqd,rejqf->edf", xs, dgu, preferred_element_type=F32)
    square = jnp.sum(grad_gu * grad_gu) + jnp.sum(grad_down * grad_down)
    tok, total = scatter_third(n_ex, n_dp, tok, jnp.full((8, 128), square, F32))
    tok_grad = jnp.transpose(tok, (1, 0, 2)).reshape(rows, width)
    mean_square = total[0, 0] / (EXPERTS * 3 * width * fw)
    return tok_grad, prob_grad, grad_gu, grad_down, mean_square


def solution(mesh):
    both = P(("dp", "expert"), None)
    weights = (P("expert", "dp", None), P("expert", None, "dp"))
    return jax.shard_map(
        body,
        mesh=mesh,
        in_specs=(both,) * 5 + (P("dp", "expert", None, None),) + weights,
        out_specs=(both, both) + weights + (P(),),
        check_vma=False,
    )
```
